32 devices in a mesh: groups: 2 (over x), gx: 16 (over z, y, core).
Axes of the slice: x: 2, y: 2, z: 4, core: 2. Of those that a mesh axis runs over, the one named last changes fastest.
Arguments:
- point_attributes: bfloat16 [16384, 128], P(('groups', 'gx')), parts along dimension 0, may hold values from -6 to 6
- kernel_matrices: bfloat16 [27, 128, 128], replicated, may hold values from -0.109375 to 0.109375
- cotangent_of_sum: bfloat16 [16384, 128], P(('groups', 'gx')), parts along dimension 0, may hold values from -6 to 6
- alive_point_counts: int32 [32], P(('groups', 'gx')), parts along dimension 0, may hold values from 64 to 512, as said below
- gather_lookup_plan: int32 [27, 16384], P(None, ('groups', 'gx')), parts along dimension 1, may hold values from -1 to 767, as said below
- export_point_lists: int32 [32, 4, 64], P(('groups', 'gx')), parts along dimension 0, may hold values from 0 to 511, as said below
Outputs:
- layer_result_vectors: bfloat16 [16384, 128], P(('groups', 'gx')), parts along dimension 0
- input_derivative: bfloat16 [16384, 128], P(('groups', 'gx')), parts along dimension 0
- grad_weight: float32 [54, 128, 128], P('groups'), parts along dimension 0
The draws below stay inside these ranges and needn't reach their ends.
There are 2 independent parts, one for each index of `groups`. The reference program is written for one: setup_inputs(seed, part) draws one part's arguments, and reference() takes and returns one part's arrays. A program takes and returns all parts, laid end to end along the dimension named above; an argument that names none is the same for every part. Nothing has to cross between parts.
Inputs may be any that keep to these rules, and one draw needn't show every extreme that they name: `alive_point_counts`: some owner holds 512 live sites and some holds 64. `export_point_lists`: every entry names a live site of the sending owner; each side's list holds 64 entries, repeats allowed. `gather_lookup_plan`: -1 means no neighbour; the middle offset of a live site names the site itself; all entries of sites at or past the owner's count are -1; values under 512 name a live site of the same owner, the others a received row of site_table.
All inputs are finite; a program needn't handle non-finite values.
Results may differ from the reference program's by a relative error of at most 0.003.
Values may be sent and summed in bfloat16 or wider, within the bound.
A program may use at most 64 MiB of HBM per device.

```python
import jax
import jax.numpy as jnp

CH = 128
OFFSETS = 27
SEATS_EACH_PART = 512
DIRS = 4
HALO = 64
ALL_SITES = 8192
N_GX = 16


def shared_counts(key):
    first, second = jax.random.split(jax.random.fold_in(key, 101))
    counted = jax.random.randint(first, (N_GX,), SEATS_EACH_PART // 8, SEATS_EACH_PART // 2 + 1)
    order = jax.random.permutation(second, N_GX)
    counted = counted.at[order[0]].set(SEATS_EACH_PART)
    counted = counted.at[order[1]].set(SEATS_EACH_PART // 8)
    return counted.astype(jnp.int32)


def draw_alive_point_counts(key, part):
    return shared_counts(key)


def draw_export_point_lists(key, part):
    counted = shared_counts(key)
    key = jax.random.fold_in(key, 23)
    chosen = jax.random.randint(key, (N_GX, DIRS, HALO), 0, counted[:, None, None])
    chosen = chosen.at[:, :, 0].set(jnp.broadcast_to(counted[:, None] - 1, (N_GX, DIRS)))
    chosen = chosen.at[:, :, 1].set(0)
    return chosen.astype(jnp.int32)


def draw_gather_lookup_plan(key, part):
    counted = shared_counts(key)
    key = jax.random.fold_in(key, 37)
    first, second, third = jax.random.split(key, 3)
    shape = (OFFSETS, N_GX, SEATS_EACH_PART)
    kinds = jax.random.randint(first, shape, 0, 10)
    local = jax.random.randint(second, shape, 0, counted[None, :, None])
    remote = jax.random.randint(third, shape, SEATS_EACH_PART, SEATS_EACH_PART + DIRS * HALO)
    rules = jnp.where(kinds < 4, -1, jnp.where(kinds < 8, local, remote))
    grid_point_locations = jnp.arange(SEATS_EACH_PART, dtype=jnp.int32)
    rules = rules.at[OFFSETS // 2].set(jnp.broadcast_to(grid_point_locations[None, :], (N_GX, SEATS_EACH_PART)))
    alive = grid_point_locations[None, None, :] < counted[None, :, None]
    rules = jnp.where(alive, rules, -1)
    rules = rules.at[0, 0, 0].set(SEATS_EACH_PART + DIRS * HALO - 1)
    rules = rules.at[1, 0, 0].set(-1)
    return rules.reshape(OFFSETS, N_GX * SEATS_EACH_PART).astype(jnp.int32)


def block_levels(rng, dims, cuts, smallest, top_value):
    loudness, own = 1.0, jax.random.fold_in(rng, 6)
    for axis_at, shards_of in cuts:
        steps = jnp.exp(jax.random.uniform(jax.random.fold_in(own, axis_at), (shards_of,), jnp.float32, smallest / len(cuts), top_value / len(cuts)))
        loudness = loudness * jnp.repeat(steps, dims[axis_at] // shards_of).reshape([-1 if axis == axis_at else 1 for axis in range(len(dims))])
    return loudness


def noise(key, shape, spread, limit, cuts=(), kind=jnp.bfloat16):
    factor_of = block_levels(key, shape, cuts, -0.22, 0.18) if cuts else 1.0
    drawn = jax.random.normal(key, shape, jnp.float32) * spread * factor_of
    return jnp.minimum(jnp.maximum(drawn, -limit), limit).astype(kind)


def setup_inputs(seed: int = 0, part: int = 0) -> dict:
    seeds = jax.random.split(jax.random.key(seed), 7)
    own_keys = jax.random.split(jax.random.fold_in(seeds[6], part), 7)
    point_attributes = noise(own_keys[0], (ALL_SITES, CH), 1.0, 6.0, ((0, 16),))
    kernel_matrices = noise(seeds[1], (OFFSETS, CH, CH), (OFFSETS * CH) ** -0.5, 0.109375)
    cotangent_of_sum = noise(own_keys[2], (ALL_SITES, CH), 1.0, 6.0, ((0, 16),))
    alive_point_counts = draw_alive_point_counts(jax.random.fold_in(jax.random.fold_in(seeds[6], part), 71), part)
    gather_lookup_plan = draw_gather_lookup_plan(jax.random.fold_in(jax.random.fold_in(seeds[6], part), 71), part)
    export_point_lists = draw_export_point_lists(jax.random.fold_in(jax.random.fold_in(seeds[6], part), 71), part)
    return {"point_attributes": point_attributes, "kernel_matrices": kernel_matrices, "cotangent_of_sum": cotangent_of_sum, "alive_point_counts": alive_point_counts, "gather_lookup_plan": gather_lookup_plan, "export_point_lists": export_point_lists}


def device_shift(stacked, distance):
    padding = jnp.zeros_like(stacked[:abs(distance)])
    if distance > 0:
        return jnp.concatenate([padding, stacked[:-distance]], axis=0)
    return jnp.concatenate([stacked[-distance:], padding], axis=0)


def side_distance(slot_index):
    return (slot_index // 2 + 1) * (1 - 2 * (slot_index % 2))


def take_rows(source, chosen):
    return source[chosen]


def add_rows(target, chosen, values):
    return target.at[chosen].add(values)


def reference(point_attributes, kernel_matrices, cotangent_of_sum, alive_point_counts, gather_lookup_plan, export_point_lists):
    input_channel_data = point_attributes.reshape(N_GX, SEATS_EACH_PART, CH)
    incoming_derivative = cotangent_of_sum.reshape(N_GX, SEATS_EACH_PART, CH).astype(jnp.float32)
    rule_rows = gather_lookup_plan.reshape(OFFSETS, N_GX, SEATS_EACH_PART)
    filled_cell_markers = (jnp.arange(SEATS_EACH_PART, dtype=jnp.int32)[None, :] < alive_point_counts[:, None]).astype(jnp.float32)[:, :, None]
    outgoing = jax.vmap(take_rows)(input_channel_data, export_point_lists)
    pieces = [input_channel_data]
    for slot_index in range(DIRS):
        pieces.append(device_shift(outgoing[:, slot_index], side_distance(slot_index)))
    pieces.append(jnp.zeros((N_GX, 1, CH), point_attributes.dtype))
    site_table = jnp.concatenate(pieces, axis=1)
    zero_row = SEATS_EACH_PART + DIRS * HALO
    row_picks = jnp.where(rule_rows < 0, zero_row, rule_rows).astype(jnp.int32)
    linear_response = jnp.zeros((N_GX * SEATS_EACH_PART, CH), jnp.float32)
    for offset in range(OFFSETS):
        gathered = jax.vmap(take_rows)(site_table, row_picks[offset]).reshape(N_GX * SEATS_EACH_PART, CH)
        linear_response = linear_response + jnp.dot(gathered, kernel_matrices[offset], preferred_element_type=jnp.float32)
    linear_response = linear_response.reshape(N_GX, SEATS_EACH_PART, CH)
    logistic_multiplier = jax.nn.sigmoid(linear_response)
    layer_result_vectors = (filled_cell_markers * (input_channel_data.astype(jnp.float32) + linear_response * logistic_multiplier)).astype(jnp.bfloat16)
    linear_response_derivative = (filled_cell_markers * incoming_derivative * logistic_multiplier * (1.0 + linear_response * (1.0 - logistic_multiplier))).astype(jnp.bfloat16)
    flat_grad = linear_response_derivative.reshape(N_GX * SEATS_EACH_PART, CH)
    table_grad = jnp.zeros((N_GX, zero_row + 1, CH), jnp.float32)
    weight_grads = []
    for offset in range(OFFSETS):
        gathered = jax.vmap(take_rows)(site_table, row_picks[offset]).reshape(N_GX * SEATS_EACH_PART, CH)
        weight_grads.append(jnp.dot(gathered.T, flat_grad, preferred_element_type=jnp.float32))
        contrib = jnp.dot(flat_grad, kernel_matrices[offset].T, preferred_element_type=jnp.float32).reshape(N_GX, SEATS_EACH_PART, CH)
        table_grad = jax.vmap(add_rows)(table_grad, row_picks[offset], contrib)
    adjacent_accumulated = incoming_derivative + table_grad[:, :SEATS_EACH_PART]
    for slot_index in range(DIRS):
        lower = SEATS_EACH_PART + slot_index * HALO
        returned = device_shift(table_grad[:, lower:lower + HALO], -side_distance(slot_index))
        adjacent_accumulated = jax.vmap(add_rows)(adjacent_accumulated, export_point_lists[:, slot_index], returned)
    input_derivative = (filled_cell_markers * adjacent_accumulated).astype(jnp.bfloat16)
    grad_weight = jnp.stack(weight_grads)
    return (layer_result_vectors.reshape(N_GX * SEATS_EACH_PART, CH), input_derivative.reshape(N_GX * SEATS_EACH_PART, CH), grad_weight)
```

```python
import functools

import jax
import jax.numpy as jnp
from jax import lax
from jax.experimental import pallas as pl
from jax.experimental.pallas import tpu as pltpu
from jax.sharding import PartitionSpec as P

BF = jnp.bfloat16
F32 = jnp.float32
MESH = pl.DeviceIdType.MESH
PIECES = 2
GROUP = 4


def side_distance(slot_index):
    return (slot_index // 2 + 1) * (1 - 2 * (slot_index % 2))


def grid_of(devices):
    chips = devices // 2
    near = 1
    while (near * 2) ** 2 <= chips and chips % (near * 2) == 0:
        near *= 2
    return near, chips // near


def rows_each(devices, padded_rows):
    share = -(-padded_rows // (PIECES * devices))
    return -(-share // 16) * 16


def kernel(
    n, r, offsets, padded,
    x_ref, w_hbm, cot_ref, cnt_ref, idx_ref, exp_ref,
    out_ref, din_ref, gw_ref,
    w_s, idx_s, t01, t2, idxb, lob, lo16, iota_s, g_s, acc, d_s, r1, s2, r2, b_s, s3, r3, og,
    hs, tacc, bs, br,
    w_sem, o_sem, hsem, hrem, bsem, brem,
    c1s, c1r, y1s, y1r, z1s, z1r, z2s, z2r, y2s, y2r, c2s, c2r,
):
    sites, ch = x_ref.shape
    sides, halo = exp_ref.shape[1], exp_ref.shape[2]
    near, far = grid_of(n)
    me = lax.axis_index("gx")
    c = lax.rem(me, 2)
    y = lax.rem(me // 2, near)
    z = me // (2 * near)
    quarter = far * r
    half = near * quarter
    low = sites // 2
    lo_rows = (sites + sides * halo) // 2

    def dev(cc, yy, zz):
        return {"gx": cc + 2 * (yy + near * zz)}

    def around(value, delta, size):
        return lax.rem(value + delta, size)

    core_peer = dev(1 - c, y, z)
    y_peers = [dev(c, around(y, k, near), z) for k in range(1, near)]
    z_peers = [dev(c, y, around(z, k, far)) for k in range(1, far)]
    fixed_peers = [core_peer] + y_peers + z_peers

    def exists(owner):
        return (owner >= 0) & (owner < n)

    barrier = pltpu.get_barrier_semaphore()
    for peer in fixed_peers:
        pl.semaphore_signal(barrier, inc=1, device_id=peer, device_id_type=MESH)
    for k in range(sides):
        owner = me + side_distance(k)

        @pl.when(exists(owner))
        def _(owner=owner):
            pl.semaphore_signal(barrier, inc=1, device_id={"gx": owner}, device_id_type=MESH)

    w_copy = pltpu.make_async_copy(w_hbm, w_s.at[pl.ds(0, offsets * ch)], w_sem)
    w_copy.start()
    w_s[pl.ds(offsets * ch, (padded - offsets) * ch), :] = jnp.zeros(
        ((padded - offsets) * ch, ch), BF
    )

    def export_picks(k):
        places = lax.broadcasted_iota(jnp.int32, (sites, halo), 0)
        return jnp.where(places == exp_ref[0, k : k + 1, :], 1.0, 0.0).astype(BF)

    for k in range(sides):
        hs[pl.ds(k * halo, halo), :] = lax.dot_general(
            export_picks(k), x_ref[...], (((0,), (0,)), ((), ())), preferred_element_type=F32
        ).astype(BF)

        @pl.when(jnp.logical_not(exists(me - side_distance(k))))
        def _(k=k):
            t2[pl.ds(k * halo, halo), :] = jnp.zeros((halo, ch), BF)

        @pl.when(jnp.logical_not(exists(me + side_distance(k))))
        def _(k=k):
            br[pl.ds(k * halo, halo), :] = jnp.zeros((halo, ch), BF)

    greeted = len(fixed_peers)
    for k in range(sides):
        greeted += jnp.where(exists(me + side_distance(k)), 1, 0)
    pl.semaphore_wait(barrier, greeted)

    def halo_copy(k):
        return pltpu.make_async_remote_copy(
            src_ref=hs.at[pl.ds(k * halo, halo)],
            dst_ref=t2.at[pl.ds(k * halo, halo)],
            send_sem=hsem.at[k],
            recv_sem=hrem.at[k],
            device_id={"gx": me + side_distance(k)},
            device_id_type=MESH,
        )

    def back_copy(k):
        return pltpu.make_async_remote_copy(
            src_ref=bs.at[pl.ds(k * halo, halo)],
            dst_ref=br.at[pl.ds(k * halo, halo)],
            send_sem=bsem.at[k],
            recv_sem=brem.at[k],
            device_id={"gx": me - side_distance(k)},
            device_id_type=MESH,
        )

    for k in range(sides):

        @pl.when(exists(me + side_distance(k)))
        def _(k=k):
            halo_copy(k).start()

    t01[:, pl.ds(0, ch)] = x_ref[pl.ds(0, low), :]
    t01[:, pl.ds(ch, ch)] = x_ref[pl.ds(low, low), :]
    idx_s[...] = jnp.full(idx_s.shape, -1.0, F32)
    idx_s[pl.ds(0, offsets), :] = idx_ref[...].astype(F32)
    rows = idx_s[...]
    lo_f = jnp.where(rows >= 2 * low, rows - 2 * low, jnp.where(rows >= low, rows - low, rows))
    lo_b = jnp.where(
        rows < 0, -1.0 * low + 1.0, jnp.where(rows >= lo_rows, rows - lo_rows, rows) - low / 2
    )
    rows_t = rows.T
    lo_t = lo_f.T
    for o in range(padded):
        idxb[o] = jnp.broadcast_to(rows_t[:, o : o + 1], (sites, ch))
        lob[o] = jnp.broadcast_to(lo_t[:, o : o + 1], (sites, ch)).astype(BF)
        lo16[o] = jnp.broadcast_to(lo_b[o : o + 1, :], (16, sites)).astype(BF)
    iota_s[...] = (
        lax.broadcasted_iota(jnp.int32, iota_s.shape, 0).astype(F32) - low / 2
    ).astype(BF)
    lanes = lax.broadcasted_iota(jnp.int32, (sites, ch), 1).astype(F32)
    lanes_a = lanes.astype(BF)
    lanes_b = (lanes + ch).astype(BF)
    one = jnp.ones((), BF)
    zero = jnp.zeros((), BF)

    def low_picks(o):
        lo = lob[o]
        return jnp.concatenate(
            [jnp.where(lo == lanes_a, one, zero), jnp.where(lo == lanes_b, one, zero)], axis=1
        )

    def own_rows(step, _):
        for i in range(GROUP):
            o = step * GROUP + i
            both = jnp.dot(low_picks(o), t01[...], preferred_element_type=F32)
            place = idxb[o]
            picked = jnp.where(
                place < low, both[:, :ch], jnp.where(place < 2 * low, both[:, ch:], 0.0)
            )
            g_s[:, pl.ds(pl.multiple_of(o * ch, ch), ch)] = picked.astype(BF)
        return 0

    lax.fori_loop(0, padded // GROUP, own_rows, 0)
    w_copy.wait()
    for k in range(sides):

        @pl.when(exists(me - side_distance(k)))
        def _(k=k):
            halo_copy(k).wait_recv()

    acc[...] = jnp.zeros_like(acc)

    def halo_rows(step, _):
        for i in range(GROUP):
            o = step * GROUP + i
            far_rows = jnp.dot(low_picks(o), t2[...], preferred_element_type=F32)
            where_o = pl.ds(pl.multiple_of(o * ch, ch), ch)
            g_s[:, where_o] = jnp.where(
                idxb[o] >= 2 * low, far_rows, g_s[:, where_o].astype(F32)
            ).astype(BF)
        span = pl.ds(pl.multiple_of(step * GROUP * ch, GROUP * ch), GROUP * ch)
        acc[...] += jnp.dot(g_s[:, span], w_s[span, :], preferred_element_type=F32)
        return 0

    lax.fori_loop(0, padded // GROUP, halo_rows, 0)

    live = jnp.where(
        lax.broadcasted_iota(jnp.int32, (sites, ch), 0) < cnt_ref[0], 1.0, 0.0
    )
    preact = acc[...]
    gate = jax.nn.sigmoid(preact)
    out_ref[...] = (live * (x_ref[...].astype(F32) + preact * gate)).astype(BF)
    pre_grad = (
        live * cot_ref[...].astype(F32) * gate * (1.0 + preact * (1.0 - gate))
    ).astype(BF)
    acc[...] = pre_grad.astype(F32)

    def weight_rows(step, _):
        span = pl.ds(pl.multiple_of(step * GROUP * ch, GROUP * ch), GROUP * ch)
        d_s[span, :] = lax.dot_general(
            g_s[:, span], acc[...].astype(BF), (((0,), (0,)), ((), ())),
            preferred_element_type=F32,
        )
        return 0

    piece = 2 * half
    extra = PIECES * piece - padded * ch
    if extra:
        d_s[pl.ds(padded * ch, extra), :] = jnp.zeros((extra, ch), F32)

    def remote(src, dst, send, recv, peer):
        return pltpu.make_async_remote_copy(
            src_ref=src, dst_ref=dst, send_sem=send, recv_sem=recv,
            device_id=peer, device_id_type=MESH,
        )

    def at(start, size):
        return pl.ds(pl.multiple_of(start, 16), size)

    def core_sum(p):
        return remote(
            d_s.at[at(p * piece + (1 - c) * half, half)], r1.at[at(p * half, half)],
            c1s.at[p], c1r.at[p], core_peer,
        )

    def y_sum(p, k):
        slot = p * (near - 1) + k
        part = at(slot * quarter, quarter)
        return remote(s2.at[part], r2.at[part], y1s.at[slot], y1r.at[slot], y_peers[k])

    def z_sum(p, k):
        slot = p * (far - 1) + k
        part = at(slot * r, r)
        return remote(s3.at[part], r3.at[part], z1s.at[slot], z1r.at[slot], z_peers[k])

    def z_share(p, k):
        slot = p * (far - 1) + k
        part = at(p * piece + c * half + y * quarter + z * r, r)
        return remote(og.at[part], og.at[part], z2s.at[slot], z2r.at[slot], z_peers[k])

    def y_share(p, k):
        slot = p * (near - 1) + k
        part = at(p * piece + c * half + y * quarter, quarter)
        return remote(og.at[part], og.at[part], y2s.at[slot], y2r.at[slot], y_peers[k])

    def core_share(p):
        part = at(p * piece + c * half, half)
        return remote(og.at[part], og.at[part], c2s.at[p], c2r.at[p], core_peer)

    def out_copy(p):
        part = pl.ds(p * piece, piece)
        return pltpu.make_async_copy(og.at[part], gw_ref.at[part], o_sem.at[p])

    def after_core(p):
        core_sum(p).wait_recv()
        for k in range(near - 1):
            yy = around(y, k + 1, near)
            s2[at((p * (near - 1) + k) * quarter, quarter), :] = (
                d_s[at(p * piece + c * half + yy * quarter, quarter), :]
                + r1[at(p * half + yy * quarter, quarter), :]
            ).astype(BF)
            y_sum(p, k).start()
        b_s[at(p * quarter, quarter), :] = (
            d_s[at(p * piece + c * half + y * quarter, quarter), :]
            + r1[at(p * half + y * quarter, quarter), :]
        )

    def after_y(p):
        for k in range(near - 1):
            y_sum(p, k).wait_recv()
        total = b_s[at(p * quarter, quarter), :]
        for k in range(near - 1):
            total += r2[at((p * (near - 1) + k) * quarter, quarter), :].astype(F32)
        b_s[at(p * quarter, quarter), :] = total
        for k in range(far - 1):
            zz = around(z, k + 1, far)
            s3[at((p * (far - 1) + k) * r, r), :] = b_s[at(p * quarter + zz * r, r), :].astype(BF)
            z_sum(p, k).start()

    def after_z(p):
        for k in range(far - 1):
            z_sum(p, k).wait_recv()
        total = b_s[at(p * quarter + z * r, r), :]
        for k in range(far - 1):
            total += r3[at((p * (far - 1) + k) * r, r), :].astype(F32)
        og[at(p * piece + c * half + y * quarter + z * r, r), :] = total.astype(BF)
        for k in range(far - 1):
            z_share(p, k).start()

    def after_z_share(p):
        for k in range(far - 1):
            z_share(p, k).wait_recv()
        for k in range(near - 1):
            y_share(p, k).start()

    def after_y_share(p):
        for k in range(near - 1):
            y_share(p, k).wait_recv()
        core_share(p).start()

    def after_core_share(p):
        core_share(p).wait_recv()
        out_copy(p).start()

    tacc[...] = jnp.zeros_like(tacc)

    def table_rows(step, _):
        span = pl.ds(pl.multiple_of(step * GROUP * ch, GROUP * ch), GROUP * ch)
        spread = lax.dot_general(
            acc[...].astype(BF), w_s[span, :], (((1,), (1,)), ((), ())),
            preferred_element_type=F32,
        )
        picks, parts = [], []
        for i in range(GROUP):
            o = step * GROUP + i
            upper = idxb[o] >= lo_rows
            term = spread[:, i * ch : (i + 1) * ch]
            parts.append(
                jnp.concatenate(
                    [jnp.where(upper, 0.0, term).astype(BF), jnp.where(upper, term, 0.0).astype(BF)],
                    axis=1,
                )
            )
            hit = iota_s[...].reshape(lo_rows // 16, 16, sites) == lo16[o][None]
            picks.append(jnp.where(hit, one, zero).reshape(lo_rows, sites))
        tacc[...] += jnp.dot(
            jnp.concatenate(picks, axis=1),
            jnp.concatenate(parts, axis=0),
            preferred_element_type=F32,
        )
        return 0

    steps = padded // GROUP
    first = -(-piece // (GROUP * ch))
    lax.fori_loop(0, min(first, steps), weight_rows, 0)
    core_sum(0).start()
    lax.fori_loop(min(first, steps), steps, weight_rows, 0)
    core_sum(1).start()
    lax.fori_loop(0, 2, table_rows, 0)
    after_core(0)
    after_core(1)
    lax.fori_loop(2, 4, table_rows, 0)
    after_y(0)
    lax.fori_loop(4, 6, table_rows, 0)
    after_y(1)
    lax.fori_loop(6, steps, table_rows, 0)
    bs[...] = tacc[pl.ds(lo_rows - sides * halo, sides * halo), pl.ds(ch, ch)].astype(BF)
    for k in range(sides):

        @pl.when(exists(me - side_distance(k)))
        def _(k=k):
            back_copy(k).start()

    after_z(0)
    after_z(1)
    after_z_share(0)
    for k in range(sides):

        @pl.when(exists(me + side_distance(k)))
        def _(k=k):
            back_copy(k).wait_recv()

    scattered = jnp.dot(export_picks(0), br[pl.ds(0, halo), :], preferred_element_type=F32)
    for k in range(1, sides):
        scattered += jnp.dot(
            export_picks(k), br[pl.ds(k * halo, halo), :], preferred_element_type=F32
        )
    own = jnp.concatenate(
        [tacc[:, pl.ds(0, ch)], tacc[pl.ds(0, sites - lo_rows), pl.ds(ch, ch)]], axis=0
    )
    din_ref[...] = (live * (cot_ref[...].astype(F32) + own + scattered)).astype(BF)
    after_z_share(1)
    after_y_share(0)
    after_y_share(1)
    after_core_share(0)
    after_core_share(1)

    for k in range(sides):

        @pl.when(exists(me + side_distance(k)))
        def _(k=k):
            halo_copy(k).wait_send()

        @pl.when(exists(me - side_distance(k)))
        def _(k=k):
            back_copy(k).wait_send()

    for p in range(PIECES):
        core_sum(p).wait_send()
        for k in range(near - 1):
            y_sum(p, k).wait_send()
            y_share(p, k).wait_send()
        for k in range(far - 1):
            z_sum(p, k).wait_send()
            z_share(p, k).wait_send()
        core_share(p).wait_send()
        out_copy(p).wait()


def body(x, w, cot, counts, plan, exports):
    n = lax.axis_size("gx")
    sites, ch = x.shape
    offsets = w.shape[0]
    padded = -(-offsets // GROUP) * GROUP
    sides, halo = exports.shape[1:]
    near, far = grid_of(n)
    r = rows_each(n, padded * ch)
    quarter = far * r
    half = near * quarter
    total = PIECES * 2 * half
    lo_rows = (sites + sides * halo) // 2
    vmem = pl.BlockSpec(memory_space=pltpu.VMEM)
    anyspace = pl.BlockSpec(memory_space=pl.ANY)
    smem = pl.BlockSpec(memory_space=pltpu.SMEM)
    dma = pltpu.SemaphoreType.DMA
    y_slots = max(1, PIECES * (near - 1))
    z_slots = max(1, PIECES * (far - 1))
    out, din, gw = pl.pallas_call(
        functools.partial(kernel, n, r, offsets, padded),
        out_shape=(
            jax.ShapeDtypeStruct((sites, ch), BF),
            jax.ShapeDtypeStruct((sites, ch), BF),
            jax.ShapeDtypeStruct((total, ch), BF),
        ),
        in_specs=[vmem, anyspace, vmem, smem, vmem, vmem],
        out_specs=(vmem, vmem, anyspace),
        scratch_shapes=[
            pltpu.VMEM((padded * ch, ch), BF),
            pltpu.VMEM((-(-padded // 8) * 8, sites), F32),
            pltpu.VMEM((sites // 2, 2 * ch), BF),
            pltpu.VMEM((sides * halo, ch), BF),
            pltpu.VMEM((padded, sites, ch), F32),
            pltpu.VMEM((padded, sites, ch), BF),
            pltpu.VMEM((padded, 16, sites), BF),
            pltpu.VMEM((lo_rows, sites), BF),
            pltpu.VMEM((sites, padded * ch), BF),
            pltpu.VMEM((sites, ch), F32),
            pltpu.VMEM((total, ch), F32),
            pltpu.VMEM((PIECES * half, ch), F32),
            pltpu.VMEM((y_slots * quarter, ch), BF),
            pltpu.VMEM((y_slots * quarter, ch), BF),
            pltpu.VMEM((PIECES * quarter, ch), F32),
            pltpu.VMEM((z_slots * r, ch), BF),
            pltpu.VMEM((z_slots * r, ch), BF),
            pltpu.VMEM((total, ch), BF),
            pltpu.VMEM((sides * halo, ch), BF),
            pltpu.VMEM((lo_rows, 2 * ch), F32),
            pltpu.VMEM((sides * halo, ch), BF),
            pltpu.VMEM((sides * halo, ch), BF),
            dma,
            dma((PIECES,)),
            dma((sides,)), dma((sides,)), dma((sides,)), dma((sides,)),
            dma((PIECES,)), dma((PIECES,)),
            dma((y_slots,)), dma((y_slots,)),
            dma((z_slots,)), dma((z_slots,)),
            dma((z_slots,)), dma((z_slots,)),
            dma((y_slots,)), dma((y_slots,)),
            dma((PIECES,)), dma((PIECES,)),
        ],
        compiler_params=pltpu.CompilerParams(
            collective_id=0, has_side_effects=True, vmem_limit_bytes=50 * 1024 * 1024
        ),
    )(x, w.reshape(offsets * ch, ch), cot, counts, plan, exports)
    grad_weight = gw[: offsets * ch].astype(F32).reshape(offsets, ch, ch)
    return out, din, grad_weight


def solution(mesh):
    return jax.shard_map(
        body,
        mesh=mesh,
        in_specs=(
            P(("groups", "gx"), None),
            P(),
            P(("groups", "gx"), None),
            P(("groups", "gx")),
            P(None, ("groups", "gx")),
            P(("groups", "gx"), None, None),
        ),
        out_specs=(P(("groups", "gx"), None), P(("groups", "gx"), None), P("groups", None, None)),
        check_vma=False,
    )
```

```python
import functools

import jax
import jax.numpy as jnp
from jax import lax
from jax.experimental import pallas as pl
from jax.experimental.pallas import tpu as pltpu
from jax.sharding import PartitionSpec as P

BF = jnp.bfloat16
F32 = jnp.float32
MESH = pl.DeviceIdType.MESH
GROUP = 4
SPAN = 4
EARLY = 4


def side_distance(slot_index):
    return (slot_index // 2 + 1) * (1 - 2 * (slot_index % 2))


def grid_of(devices):
    chips = devices // 2
    near = 1
    while (near * 2) ** 2 <= chips and chips % (near * 2) == 0:
        near *= 2
    return near, chips // near


def pieces_of(devices, padded_rows):
    for pieces in (2,):
        if padded_rows % (pieces * devices * 16) == 0:
            return pieces
    return 1


def rows_each(devices, padded_rows):
    share = -(-padded_rows // (pieces_of(devices, padded_rows) * devices))
    return -(-share // 16) * 16


def finish(
    cuts, out_in, din_in, gw_in, out_ref, din_ref, gw_ref, rows, held, wide, row_in, row_out, in_sem, out_sem
):
    size = held.shape[0] // cuts
    spans = [pl.ds(i * size, size) for i in range(cuts)]
    fetch = [pltpu.make_async_copy(gw_in.at[s], held.at[s], in_sem.at[i]) for i, s in enumerate(spans)]
    store = [pltpu.make_async_copy(wide.at[s], gw_ref.at[s], out_sem.at[i]) for i, s in enumerate(spans)]
    into = [
        pltpu.make_async_copy(source, rows.at[i], row_in.at[i]) for i, source in enumerate((out_in, din_in))
    ]
    away = [
        pltpu.make_async_copy(rows.at[i], to, row_out.at[i]) for i, to in enumerate((out_ref, din_ref))
    ]
    for copy in fetch + into:
        copy.start()
    for i, s in enumerate(spans):
        fetch[i].wait()
        wide[s, :] = held[s, :].astype(F32)
        store[i].start()
    for i in range(2):
        into[i].wait()
        away[i].start()
    for copy in store + away:
        copy.wait()


def kernel(
    n, r, offsets, padded,
    x_hbm, w_hbm, cot_hbm, cnt_hbm, idx_hbm, exp_hbm,
    out_hbm, din_hbm, gw_ref,
    x_ref, cot_ref, idx_ref, exp_ref, out_ref, din_ref, in_sem, res_sem,
    w_s, idx_s, t01, t2, idxb, lob, lo16, iota_s, g_s, acc, d_s, r1, s2, r2, b_s, s3, r3, og,
    hs, tacc, bs, br, pre_s,
    w_sem, o_sem, hsem, hrem, bsem, brem,
    c1s, c1r, y1s, y1r, z1s, z1r, z2s, z2r, y2s, y2r, c2s, c2r,
):
    sites, ch = x_ref.shape
    sides, halo = exp_ref.shape[1], exp_ref.shape[2]
    near, far = grid_of(n)
    me = lax.axis_index("gx")
    c = lax.rem(me, 2)
    y = lax.rem(me // 2, near)
    z = me // (2 * near)
    quarter = far * r
    half = near * quarter
    low = sites // 2
    others = offsets - 1
    middle = offsets // 2
    PIECES = pieces_of(n, padded * ch)
    lo_rows = (sites + sides * halo) // 2

    def dev(cc, yy, zz):
        return {"gx": cc + 2 * (yy + near * zz)}

    def around(value, delta, size):
        return lax.rem(value + delta, size)

    core_peer = dev(1 - c, y, z)
    y_peers = [dev(c, around(y, k, near), z) for k in range(1, near)]
    z_peers = [dev(c, y, around(z, k, far)) for k in range(1, far)]
    fixed_peers = [core_peer] + y_peers + z_peers

    def exists(owner):
        return (owner >= 0) & (owner < n)

    barrier = pltpu.get_barrier_semaphore()
    for peer in fixed_peers:
        pl.semaphore_signal(barrier, inc=1, device_id=peer, device_id_type=MESH)
    for k in range(sides):
        owner = me + side_distance(k)

        @pl.when(exists(owner))
        def _(owner=owner):
            pl.semaphore_signal(barrier, inc=1, device_id={"gx": owner}, device_id_type=MESH)

    w_copies = [
        pltpu.make_async_copy(
            w_hbm.at[pl.ds(source * ch, count * ch)], w_s.at[pl.ds(to * ch, count * ch)], w_sem.at[i]
        )
        for i, (source, to, count) in enumerate(
            ((0, 0, middle), (middle + 1, middle, middle), (middle, others, 1))
        )
    ]
    loads = [
        pltpu.make_async_copy(source, to, in_sem.at[i])
        for i, (source, to) in enumerate(
            ((idx_hbm, idx_ref), (x_hbm, x_ref), (exp_hbm, exp_ref), (cot_hbm, cot_ref))
        )
    ]
    for copy in loads + w_copies:
        copy.start()
    w_s[pl.ds(offsets * ch, (padded - offsets) * ch), :] = jnp.zeros(
        ((padded - offsets) * ch, ch), BF
    )

    loads[0].wait()
    idx_s[...] = jnp.full(idx_s.shape, -1.0, F32)
    idx_s[pl.ds(0, middle), :] = idx_ref[pl.ds(0, middle), :].astype(F32)
    idx_s[pl.ds(middle, middle), :] = idx_ref[pl.ds(middle + 1, middle), :].astype(F32)
    idx_s[pl.ds(others, 1), :] = idx_ref[pl.ds(middle, 1), :].astype(F32)
    rows = idx_s[...]
    lo_f = jnp.where(rows >= 2 * low, rows - 2 * low, jnp.where(rows >= low, rows - low, rows))
    lo_b = jnp.where(
        rows < 0, -1.0 * low + 1.0, jnp.where(rows >= lo_rows, rows - lo_rows, rows) - low / 2
    )
    rows_t = rows.T
    lo_t = lo_f.T
    for o in range(offsets):
        idxb[o] = jnp.broadcast_to(rows_t[:, o : o + 1], (sites, ch))
        lob[o] = jnp.broadcast_to(lo_t[:, o : o + 1], (sites, ch)).astype(BF)
        lo16[o] = jnp.broadcast_to(lo_b[o : o + 1, :], (16, sites)).astype(BF)
    loads[1].wait()
    loads[2].wait()
    def export_picks(k):
        places = lax.broadcasted_iota(jnp.int32, (sites, halo), 0)
        return jnp.where(places == exp_ref[0, k : k + 1, :], 1.0, 0.0).astype(BF)

    for k in range(sides):
        hs[pl.ds(k * halo, halo), :] = lax.dot_general(
            export_picks(k), x_ref[...], (((0,), (0,)), ((), ())), preferred_element_type=F32
        ).astype(BF)

        @pl.when(jnp.logical_not(exists(me - side_distance(k))))
        def _(k=k):
            t2[pl.ds(k * halo, halo), :] = jnp.zeros((halo, ch), BF)

        @pl.when(jnp.logical_not(exists(me + side_distance(k))))
        def _(k=k):
            br[pl.ds(k * halo, halo), :] = jnp.zeros((halo, ch), BF)

    def halo_copy(k):
        return pltpu.make_async_remote_copy(
            src_ref=hs.at[pl.ds(k * halo, halo)],
            dst_ref=t2.at[pl.ds(k * halo, halo)],
            send_sem=hsem.at[k],
            recv_sem=hrem.at[k],
            device_id={"gx": me + side_distance(k)},
            device_id_type=MESH,
        )

    def back_copy(k):
        return pltpu.make_async_remote_copy(
            src_ref=bs.at[pl.ds(k * halo, halo)],
            dst_ref=br.at[pl.ds(k * halo, halo)],
            send_sem=bsem.at[k],
            recv_sem=brem.at[k],
            device_id={"gx": me - side_distance(k)},
            device_id_type=MESH,
        )

    t01[:, pl.ds(0, ch)] = x_ref[pl.ds(0, low), :]
    t01[:, pl.ds(ch, ch)] = x_ref[pl.ds(low, low), :]
    iota_s[...] = (
        lax.broadcasted_iota(jnp.int32, iota_s.shape, 0).astype(F32) - low / 2
    ).astype(BF)
    lanes = lax.broadcasted_iota(jnp.int32, (sites, ch), 1).astype(F32)
    lanes_a = lanes.astype(BF)
    lanes_b = (lanes + ch).astype(BF)
    one = jnp.ones((), BF)
    zero = jnp.zeros((), BF)

    def low_picks(o):
        lo = lob[o]
        return jnp.concatenate(
            [jnp.where(lo == lanes_a, one, zero), jnp.where(lo == lanes_b, one, zero)], axis=1
        )

    live = jnp.where(idxb[others] >= 0, 1.0, 0.0)
    g_s[:, pl.ds(others * ch, ch)] = (live * x_ref[...].astype(F32)).astype(BF)
    g_s[:, pl.ds(offsets * ch, (padded - offsets) * ch)] = jnp.zeros(
        (sites, (padded - offsets) * ch), BF
    )

    def each_span(rows, first, last):
        whole = (last - first) // SPAN
        lax.fori_loop(0, whole, lambda step, _: rows(first + step * SPAN, SPAN), 0)
        if (last - first) % SPAN:
            rows(first + whole * SPAN, (last - first) % SPAN)

    def own_rows(start, count):
        for i in range(count):
            o = start + i
            both = jnp.dot(low_picks(o), t01[...], preferred_element_type=F32)
            place = idxb[o]
            picked = jnp.where(
                place < low, both[:, :ch], jnp.where(place < 2 * low, both[:, ch:], 0.0)
            )
            g_s[:, pl.ds(pl.multiple_of(o * ch, ch), ch)] = picked.astype(BF)
        return 0

    each_span(own_rows, 0, EARLY)
    greeted = len(fixed_peers)
    for k in range(sides):
        greeted += jnp.where(exists(me + side_distance(k)), 1, 0)
    pl.semaphore_wait(barrier, greeted)

    for k in range(sides):

        @pl.when(exists(me + side_distance(k)))
        def _(k=k):
            halo_copy(k).start()

    each_span(own_rows, EARLY, others)
    for copy in w_copies:
        copy.wait()
    for k in range(sides):

        @pl.when(exists(me - side_distance(k)))
        def _(k=k):
            halo_copy(k).wait_recv()

    acc[...] = jnp.dot(
        g_s[:, pl.ds(others * ch, ch)], w_s[pl.ds(others * ch, ch), :], preferred_element_type=F32
    )

    def halo_rows(start, count):
        for i in range(count):
            o = start + i
            far_rows = jnp.dot(low_picks(o), t2[...], preferred_element_type=F32)
            where_o = pl.ds(pl.multiple_of(o * ch, ch), ch)
            g_s[:, where_o] = jnp.where(
                idxb[o] >= 2 * low, far_rows, g_s[:, where_o].astype(F32)
            ).astype(BF)
        span = pl.ds(pl.multiple_of(start * ch, ch), count * ch)
        acc[...] += jnp.dot(g_s[:, span], w_s[span, :], preferred_element_type=F32)
        return 0

    each_span(halo_rows, 0, others)
    loads[3].wait()

    preact = acc[...]
    gate = jax.nn.sigmoid(preact)
    out_ref[...] = (live * (x_ref[...].astype(F32) + preact * gate)).astype(BF)
    out_copy_rows = pltpu.make_async_copy(out_ref, out_hbm, res_sem.at[0])
    out_copy_rows.start()
    pre_grad = (
        live * cot_ref[...].astype(F32) * gate * (1.0 + preact * (1.0 - gate))
    ).astype(BF)
    pre_s[...] = pre_grad

    def weight_rows(step, _):
        span = pl.ds(pl.multiple_of(step * GROUP * ch, GROUP * ch), GROUP * ch)
        d_s[span, :] = lax.dot_general(
            g_s[:, span], pre_s[...], (((0,), (0,)), ((), ())),
            preferred_element_type=F32,
        )
        return 0

    piece = 2 * half
    extra = PIECES * piece - padded * ch
    if extra:
        d_s[pl.ds(padded * ch, extra), :] = jnp.zeros((extra, ch), F32)

    def remote(src, dst, send, recv, peer):
        return pltpu.make_async_remote_copy(
            src_ref=src, dst_ref=dst, send_sem=send, recv_sem=recv,
            device_id=peer, device_id_type=MESH,
        )

    def at(start, size):
        return pl.ds(pl.multiple_of(start, 16), size)

    def core_sum(p):
        return remote(
            d_s.at[at(p * piece + (1 - c) * half, half)], r1.at[at(p * half, half)],
            c1s.at[p], c1r.at[p], core_peer,
        )

    def y_sum(p, k):
        slot = p * (near - 1) + k
        part = at(slot * quarter, quarter)
        return remote(s2.at[part], r2.at[part], y1s.at[slot], y1r.at[slot], y_peers[k])

    def z_sum(p, k):
        slot = p * (far - 1) + k
        part = at(slot * r, r)
        return remote(s3.at[part], r3.at[part], z1s.at[slot], z1r.at[slot], z_peers[k])

    def z_share(p, k):
        slot = p * (far - 1) + k
        part = at(p * piece + c * half + y * quarter + z * r, r)
        return remote(og.at[part], og.at[part], z2s.at[slot], z2r.at[slot], z_peers[k])

    def y_share(p, k):
        slot = p * (near - 1) + k
        part = at(p * piece + c * half + y * quarter, quarter)
        return remote(og.at[part], og.at[part], y2s.at[slot], y2r.at[slot], y_peers[k])

    def core_share(p):
        part = at(p * piece + c * half, half)
        return remote(og.at[part], og.at[part], c2s.at[p], c2r.at[p], core_peer)

    def out_copies(p):
        copies = []
        for source, to, count in (
            (0, 0, middle), (middle, middle + 1, middle), (others, middle, 1)
        ):
            first, last = max(source * ch, p * piece), min((source + count) * ch, (p + 1) * piece)
            if first < last:
                copies.append(
                    pltpu.make_async_copy(
                        og.at[pl.ds(first, last - first)],
                        gw_ref.at[pl.ds(first + (to - source) * ch, last - first)],
                        o_sem.at[3 * p + len(copies)],
                    )
                )
        return copies

    def after_core(p):
        core_sum(p).wait_recv()
        for k in range(near - 1):
            yy = around(y, k + 1, near)
            s2[at((p * (near - 1) + k) * quarter, quarter), :] = (
                d_s[at(p * piece + c * half + yy * quarter, quarter), :]
                + r1[at(p * half + yy * quarter, quarter), :]
            ).astype(BF)
            y_sum(p, k).start()
        b_s[at(p * quarter, quarter), :] = (
            d_s[at(p * piece + c * half + y * quarter, quarter), :]
            + r1[at(p * half + y * quarter, quarter), :]
        )

    def after_y(p):
        for k in range(near - 1):
            y_sum(p, k).wait_recv()
        total = b_s[at(p * quarter, quarter), :]
        for k in range(near - 1):
            total += r2[at((p * (near - 1) + k) * quarter, quarter), :].astype(F32)
        b_s[at(p * quarter, quarter), :] = total
        for k in range(far - 1):
            zz = around(z, k + 1, far)
            s3[at((p * (far - 1) + k) * r, r), :] = b_s[at(p * quarter + zz * r, r), :].astype(BF)
            z_sum(p, k).start()

    def after_z(p):
        for k in range(far - 1):
            z_sum(p, k).wait_recv()
        total = b_s[at(p * quarter + z * r, r), :]
        for k in range(far - 1):
            total += r3[at((p * (far - 1) + k) * r, r), :].astype(F32)
        og[at(p * piece + c * half + y * quarter + z * r, r), :] = total.astype(BF)
        for k in range(far - 1):
            z_share(p, k).start()

    def after_z_share(p):
        for k in range(far - 1):
            z_share(p, k).wait_recv()
        for k in range(near - 1):
            y_share(p, k).start()

    def after_y_share(p):
        for k in range(near - 1):
            y_share(p, k).wait_recv()
        core_share(p).start()

    def after_core_share(p):
        core_share(p).wait_recv()
        for copy in out_copies(p):
            copy.start()

    tacc[...] = jnp.zeros_like(tacc)

    def table_rows(start, count):
        span = pl.ds(pl.multiple_of(start * ch, ch), count * ch)
        spread = lax.dot_general(
            pre_s[...], w_s[span, :], (((1,), (1,)), ((), ())), preferred_element_type=F32
        )
        picks, parts = [], []
        for i in range(count):
            o = start + i
            upper = idxb[o] >= lo_rows
            term = spread[:, i * ch : (i + 1) * ch]
            parts.append(
                jnp.concatenate(
                    [jnp.where(upper, 0.0, term).astype(BF), jnp.where(upper, term, 0.0).astype(BF)],
                    axis=1,
                )
            )
            hit = iota_s[...].reshape(lo_rows // 16, 16, sites) == lo16[o][None]
            picks.append(jnp.where(hit, one, zero).reshape(lo_rows, sites))
        tacc[...] += jnp.dot(
            jnp.concatenate(picks, axis=1),
            jnp.concatenate(parts, axis=0),
            preferred_element_type=F32,
        )
        return 0

    def send_back():
        bs[...] = tacc[pl.ds(lo_rows - sides * halo, sides * halo), pl.ds(ch, ch)].astype(BF)
        for k in range(sides):

            @pl.when(exists(me - side_distance(k)))
            def _(k=k):
                back_copy(k).start()

    def finish_rows():
        for k in range(sides):

            @pl.when(exists(me + side_distance(k)))
            def _(k=k):
                back_copy(k).wait_recv()

        scattered = lax.dot_general(
            pre_s[...], w_s[pl.ds(others * ch, ch), :], (((1,), (1,)), ((), ())),
            preferred_element_type=F32,
        )
        for k in range(sides):
            scattered += jnp.dot(
                export_picks(k), br[pl.ds(k * halo, halo), :], preferred_element_type=F32
            )
        own = jnp.concatenate(
            [tacc[:, pl.ds(0, ch)], tacc[pl.ds(0, sites - lo_rows), pl.ds(ch, ch)]], axis=0
        )
        alive = jnp.where(idxb[others] >= 0, 1.0, 0.0)
        din_ref[...] = (alive * (cot_ref[...].astype(F32) + own + scattered)).astype(BF)
        pltpu.make_async_copy(din_ref, din_hbm, res_sem.at[1]).start()

    steps = padded // GROUP
    done = 0
    for p in range(PIECES):
        need = min(steps, -(-(p + 1) * piece // (GROUP * ch)))
        if need > done:
            lax.fori_loop(done, need, weight_rows, 0)
            done = need
        core_sum(p).start()
    for p in range(PIECES):
        after_core(p)
    cuts = [min(others, cut) for cut in (12, 20, others)]
    each_span(table_rows, 0, cuts[0])
    after_y(0)
    each_span(table_rows, cuts[0], cuts[1])
    for p in range(1, PIECES):
        after_y(p)
    each_span(table_rows, cuts[1], cuts[2])
    send_back()
    for p in range(PIECES):
        after_z(p)
    after_z_share(0)
    finish_rows()
    for p in range(1, PIECES):
        after_z_share(p)
    for p in range(PIECES):
        after_y_share(p)
    for p in range(PIECES):
        after_core_share(p)

    for k in range(sides):

        @pl.when(exists(me + side_distance(k)))
        def _(k=k):
            halo_copy(k).wait_send()

        @pl.when(exists(me - side_distance(k)))
        def _(k=k):
            back_copy(k).wait_send()

    for p in range(PIECES):
        core_sum(p).wait_send()
        for k in range(near - 1):
            y_sum(p, k).wait_send()
            y_share(p, k).wait_send()
        for k in range(far - 1):
            z_sum(p, k).wait_send()
            z_share(p, k).wait_send()
        core_share(p).wait_send()
        for copy in out_copies(p):
            copy.wait()
    out_copy_rows.wait()
    pltpu.make_async_copy(din_ref, din_hbm, res_sem.at[1]).wait()


def body(x, w, cot, counts, plan, exports):
    n = lax.axis_size("gx")
    sites, ch = x.shape
    offsets = w.shape[0]
    padded = -(-offsets // GROUP) * GROUP
    sides, halo = exports.shape[1:]
    middle = offsets // 2
    near, far = grid_of(n)
    r = rows_each(n, padded * ch)
    quarter = far * r
    half = near * quarter
    pieces = pieces_of(n, padded * ch)
    total = pieces * 2 * half
    lo_rows = (sites + sides * halo) // 2
    anyspace = pl.BlockSpec(memory_space=pl.ANY)
    dma = pltpu.SemaphoreType.DMA
    y_slots = max(1, pieces * (near - 1))
    z_slots = max(1, pieces * (far - 1))
    out, din, gw = pl.pallas_call(
        functools.partial(kernel, n, r, offsets, padded),
        out_shape=(
            jax.ShapeDtypeStruct((sites, ch), BF),
            jax.ShapeDtypeStruct((sites, ch), BF),
            jax.ShapeDtypeStruct((offsets * ch, ch), BF),
        ),
        in_specs=[anyspace] * 6,
        out_specs=(anyspace,) * 3,
        scratch_shapes=[
            pltpu.VMEM((sites, ch), BF),
            pltpu.VMEM((sites, ch), BF),
            pltpu.VMEM((offsets, sites), jnp.int32),
            pltpu.VMEM((1, sides, halo), jnp.int32),
            pltpu.VMEM((sites, ch), BF),
            pltpu.VMEM((sites, ch), BF),
            dma((4,)),
            dma((2,)),
            pltpu.VMEM((padded * ch, ch), BF),
            pltpu.VMEM((-(-padded // 8) * 8, sites), F32),
            pltpu.VMEM((sites // 2, 2 * ch), BF),
            pltpu.VMEM((sides * halo, ch), BF),
            pltpu.VMEM((padded, sites, ch), F32),
            pltpu.VMEM((padded, sites, ch), BF),
            pltpu.VMEM((padded, 16, sites), BF),
            pltpu.VMEM((lo_rows, sites), BF),
            pltpu.VMEM((sites, padded * ch), BF),
            pltpu.VMEM((sites, ch), F32),
            pltpu.VMEM((total, ch), F32),
            pltpu.VMEM((pieces * half, ch), F32),
            pltpu.VMEM((y_slots * quarter, ch), BF),
            pltpu.VMEM((y_slots * quarter, ch), BF),
            pltpu.VMEM((pieces * quarter, ch), F32),
            pltpu.VMEM((z_slots * r, ch), BF),
            pltpu.VMEM((z_slots * r, ch), BF),
            pltpu.VMEM((total, ch), BF),
            pltpu.VMEM((sides * halo, ch), BF),
            pltpu.VMEM((lo_rows, 2 * ch), F32),
            pltpu.VMEM((sides * halo, ch), BF),
            pltpu.VMEM((sides * halo, ch), BF),
            pltpu.VMEM((sites, ch), BF),
            dma((3,)),
            dma((3 * pieces,)),
            dma((sides,)), dma((sides,)), dma((sides,)), dma((sides,)),
            dma((pieces,)), dma((pieces,)),
            dma((y_slots,)), dma((y_slots,)),
            dma((z_slots,)), dma((z_slots,)),
            dma((z_slots,)), dma((z_slots,)),
            dma((y_slots,)), dma((y_slots,)),
            dma((pieces,)), dma((pieces,)),
        ],
        compiler_params=pltpu.CompilerParams(
            collective_id=0, has_side_effects=True, vmem_limit_bytes=60 * 1024 * 1024
        ),
    )(x, w.reshape(offsets * ch, ch), cot, counts, plan, exports)
    out, din, gw = pl.pallas_call(
        functools.partial(finish, 3),
        out_shape=(
            jax.ShapeDtypeStruct((sites, ch), BF),
            jax.ShapeDtypeStruct((sites, ch), BF),
            jax.ShapeDtypeStruct((offsets * ch, ch), F32),
        ),
        in_specs=[anyspace] * 3,
        out_specs=(anyspace,) * 3,
        scratch_shapes=[
            pltpu.VMEM((2, sites, ch), BF),
            pltpu.VMEM((offsets * ch, ch), BF),
            pltpu.VMEM((offsets * ch, ch), F32),
            dma((2,)), dma((2,)), dma((3,)), dma((3,)),
        ],
        compiler_params=pltpu.CompilerParams(vmem_limit_bytes=60 * 1024 * 1024),
    )(out, din, gw)
    return out, din, gw.reshape(offsets, ch, ch)


def solution(mesh):
    return jax.shard_map(
        body,
        mesh=mesh,
        in_specs=(
            P(("groups", "gx"), None),
            P(),
            P(("groups", "gx"), None),
            P(("groups", "gx")),
            P(None, ("groups", "gx")),
            P(("groups", "gx"), None, None),
        ),
        out_specs=(P(("groups", "gx"), None), P(("groups", "gx"), None), P("groups", None, None)),
        check_vma=False,
    )
```

```python
import functools

import jax
import jax.numpy as jnp
from jax import lax
from jax.experimental import pallas as pl
from jax.experimental.pallas import tpu as pltpu
from jax.sharding import PartitionSpec as P

BF = jnp.bfloat16
F32 = jnp.float32
MESH = pl.DeviceIdType.MESH
GROUP = 4
SPAN = 4


def side_distance(slot_index):
    return (slot_index // 2 + 1) * (1 - 2 * (slot_index % 2))


def grid_of(devices):
    chips = devices // 2
    near = 1
    while (near * 2) ** 2 <= chips and chips % (near * 2) == 0:
        near *= 2
    return near, chips // near


def pieces_of(devices, padded_rows):
    for pieces in (2,):
        if padded_rows % (pieces * devices * 16) == 0:
            return pieces
    return 1


def rows_each(devices, padded_rows):
    share = -(-padded_rows // (pieces_of(devices, padded_rows) * devices))
    return -(-share // 16) * 16


def finish(
    cuts, out_in, din_in, gw_in, out_ref, din_ref, gw_ref, rows, held, wide, row_in, row_out, in_sem, out_sem
):
    size = held.shape[0] // cuts
    spans = [pl.ds(i * size, size) for i in range(cuts)]
    fetch = [pltpu.make_async_copy(gw_in.at[s], held.at[s], in_sem.at[i]) for i, s in enumerate(spans)]
    store = [pltpu.make_async_copy(wide.at[s], gw_ref.at[s], out_sem.at[i]) for i, s in enumerate(spans)]
    into = [
        pltpu.make_async_copy(source, rows.at[i], row_in.at[i]) for i, source in enumerate((out_in, din_in))
    ]
    away = [
        pltpu.make_async_copy(rows.at[i], to, row_out.at[i]) for i, to in enumerate((out_ref, din_ref))
    ]
    for copy in fetch + into:
        copy.start()
    for i, s in enumerate(spans):
        fetch[i].wait()
        wide[s, :] = held[s, :].astype(F32)
        store[i].start()
    for i in range(2):
        into[i].wait()
        away[i].start()
    for copy in store + away:
        copy.wait()


def kernel(
    n, r, offsets, padded,
    x_hbm, w_hbm, cot_hbm, cnt_hbm, idx_hbm, exp_hbm,
    out_hbm, din_hbm, gw_ref,
    x_ref, cot_ref, idx_ref, exp_ref, out_ref, din_ref, in_sem, res_sem,
    w_s, idx_s, t01, t2, idxb, lob, lo16, iota_s, g_s, acc, d_s, r1, s2, r2, b_s, s3, r3, og,
    hs, tacc, bs, br, pre_s,
    w_sem, o_sem, hsem, hrem, bsem, brem,
    c1s, c1r, y1s, y1r, z1s, z1r, z2s, z2r, y2s, y2r, c2s, c2r,
):
    sites, ch = x_ref.shape
    sides, halo = exp_ref.shape[1], exp_ref.shape[2]
    near, far = grid_of(n)
    me = lax.axis_index("gx")
    c = lax.rem(me, 2)
    y = lax.rem(me // 2, near)
    z = me // (2 * near)
    quarter = far * r
    half = near * quarter
    low = sites // 2
    others = offsets - 1
    middle = offsets // 2
    PIECES = pieces_of(n, padded * ch)
    lo_rows = (sites + sides * halo) // 2

    def dev(cc, yy, zz):
        return {"gx": cc + 2 * (yy + near * zz)}

    def around(value, delta, size):
        return lax.rem(value + delta, size)

    core_peer = dev(1 - c, y, z)
    y_peers = [dev(c, around(y, k, near), z) for k in range(1, near)]
    z_peers = [dev(c, y, around(z, k, far)) for k in range(1, far)]
    fixed_peers = [core_peer] + y_peers + z_peers

    def exists(owner):
        return (owner >= 0) & (owner < n)

    barrier = pltpu.get_barrier_semaphore()
    for peer in fixed_peers:
        pl.semaphore_signal(barrier, inc=1, device_id=peer, device_id_type=MESH)
    for k in range(sides):
        owner = me + side_distance(k)

        @pl.when(exists(owner))
        def _(owner=owner):
            pl.semaphore_signal(barrier, inc=1, device_id={"gx": owner}, device_id_type=MESH)

    w_copies = [
        pltpu.make_async_copy(
            w_hbm.at[pl.ds(source * ch, count * ch)], w_s.at[pl.ds(to * ch, count * ch)], w_sem.at[i]
        )
        for i, (source, to, count) in enumerate(
            ((0, 0, middle), (middle + 1, middle, middle), (middle, others, 1))
        )
    ]
    loads = [
        pltpu.make_async_copy(source, to, in_sem.at[i])
        for i, (source, to) in enumerate(
            ((idx_hbm, idx_ref), (x_hbm, x_ref), (exp_hbm, exp_ref), (cot_hbm, cot_ref))
        )
    ]
    for copy in loads + w_copies:
        copy.start()
    w_s[pl.ds(offsets * ch, (padded - offsets) * ch), :] = jnp.zeros(
        ((padded - offsets) * ch, ch), BF
    )

    loads[0].wait()
    idx_s[...] = jnp.full(idx_s.shape, -1.0, F32)
    idx_s[pl.ds(0, middle), :] = idx_ref[pl.ds(0, middle), :].astype(F32)
    idx_s[pl.ds(middle, middle), :] = idx_ref[pl.ds(middle + 1, middle), :].astype(F32)
    idx_s[pl.ds(others, 1), :] = idx_ref[pl.ds(middle, 1), :].astype(F32)
    rows = idx_s[...]
    lo_f = jnp.where(rows >= 2 * low, rows - 2 * low, jnp.where(rows >= low, rows - low, rows))
    lo_b = jnp.where(
        rows < 0, -1.0 * low + 1.0, jnp.where(rows >= lo_rows, rows - lo_rows, rows) - low / 2
    )
    rows_t = rows.T
    lo_t = lo_f.T
    for o in range(offsets):
        idxb[o] = jnp.broadcast_to(rows_t[:, o : o + 1], (sites, ch))
        lob[o] = jnp.broadcast_to(lo_t[:, o : o + 1], (sites, ch)).astype(BF)
        lo16[o] = jnp.broadcast_to(lo_b[o : o + 1, :], (16, sites)).astype(BF)
    loads[1].wait()
    loads[2].wait()
    def export_picks(k):
        places = lax.broadcasted_iota(jnp.int32, (sites, halo), 0)
        return jnp.where(places == exp_ref[0, k : k + 1, :], 1.0, 0.0).astype(BF)

    for k in range(sides):
        hs[pl.ds(k * halo, halo), :] = lax.dot_general(
            export_picks(k), x_ref[...], (((0,), (0,)), ((), ())), preferred_element_type=F32
        ).astype(BF)

        @pl.when(jnp.logical_not(exists(me - side_distance(k))))
        def _(k=k):
            t2[pl.ds(k * halo, halo), :] = jnp.zeros((halo, ch), BF)

        @pl.when(jnp.logical_not(exists(me + side_distance(k))))
        def _(k=k):
            br[pl.ds(k * halo, halo), :] = jnp.zeros((halo, ch), BF)

    def halo_copy(k):
        return pltpu.make_async_remote_copy(
            src_ref=hs.at[pl.ds(k * halo, halo)],
            dst_ref=t2.at[pl.ds(k * halo, halo)],
            send_sem=hsem.at[k],
            recv_sem=hrem.at[k],
            device_id={"gx": me + side_distance(k)},
            device_id_type=MESH,
        )

    def back_copy(k):
        return pltpu.make_async_remote_copy(
            src_ref=bs.at[pl.ds(k * halo, halo)],
            dst_ref=br.at[pl.ds(k * halo, halo)],
            send_sem=bsem.at[k],
            recv_sem=brem.at[k],
            device_id={"gx": me - side_distance(k)},
            device_id_type=MESH,
        )

    t01[:, pl.ds(0, ch)] = x_ref[pl.ds(0, low), :]
    t01[:, pl.ds(ch, ch)] = x_ref[pl.ds(low, low), :]
    iota_s[...] = (
        lax.broadcasted_iota(jnp.int32, iota_s.shape, 0).astype(F32) - low / 2
    ).astype(BF)
    lanes = lax.broadcasted_iota(jnp.int32, (sites, ch), 1).astype(F32)
    lanes_a = lanes.astype(BF)
    lanes_b = (lanes + ch).astype(BF)
    one = jnp.ones((), BF)
    zero = jnp.zeros((), BF)

    def low_picks(o):
        lo = lob[o]
        return jnp.concatenate(
            [jnp.where(lo == lanes_a, one, zero), jnp.where(lo == lanes_b, one, zero)], axis=1
        )

    live = jnp.where(idxb[others] >= 0, 1.0, 0.0)
    g_s[:, pl.ds(others * ch, ch)] = (live * x_ref[...].astype(F32)).astype(BF)
    g_s[:, pl.ds(offsets * ch, (padded - offsets) * ch)] = jnp.zeros(
        (sites, (padded - offsets) * ch), BF
    )

    def each_span(rows, first, last, span=SPAN):
        whole = (last - first) // span
        lax.fori_loop(0, whole, lambda step, _: rows(first + step * span, span), 0)
        if (last - first) % span:
            rows(first + whole * span, (last - first) % span)

    def own_rows(start, count):
        for i in range(count):
            o = start + i
            both = jnp.dot(low_picks(o), t01[...], preferred_element_type=F32)
            place = idxb[o]
            picked = jnp.where(
                place < low, both[:, :ch], jnp.where(place < 2 * low, both[:, ch:], 0.0)
            )
            g_s[:, pl.ds(pl.multiple_of(o * ch, ch), ch)] = picked.astype(BF)
        return 0

    greeted = len(fixed_peers)
    for k in range(sides):
        greeted += jnp.where(exists(me + side_distance(k)), 1, 0)
    pl.semaphore_wait(barrier, greeted)

    for k in range(sides):

        @pl.when(exists(me + side_distance(k)))
        def _(k=k):
            halo_copy(k).start()

    each_span(own_rows, 0, others)
    for copy in w_copies:
        copy.wait()
    for k in range(sides):

        @pl.when(exists(me - side_distance(k)))
        def _(k=k):
            halo_copy(k).wait_recv()

    acc[...] = jnp.dot(
        g_s[:, pl.ds(others * ch, ch)], w_s[pl.ds(others * ch, ch), :], preferred_element_type=F32
    )

    def halo_rows(start, count):
        for i in range(count):
            o = start + i
            far_rows = jnp.dot(low_picks(o), t2[...], preferred_element_type=F32)
            where_o = pl.ds(pl.multiple_of(o * ch, ch), ch)
            g_s[:, where_o] = jnp.where(
                idxb[o] >= 2 * low, far_rows, g_s[:, where_o].astype(F32)
            ).astype(BF)
        span = pl.ds(pl.multiple_of(start * ch, ch), count * ch)
        acc[...] += jnp.dot(g_s[:, span], w_s[span, :], preferred_element_type=F32)
        return 0

    each_span(halo_rows, 0, others, 13 if others % 13 == 0 else SPAN)
    loads[3].wait()

    preact = acc[...]
    gate = jax.nn.sigmoid(preact)
    out_ref[...] = (live * (x_ref[...].astype(F32) + preact * gate)).astype(BF)
    out_copy_rows = pltpu.make_async_copy(out_ref, out_hbm, res_sem.at[0])
    out_copy_rows.start()
    pre_grad = (
        live * cot_ref[...].astype(F32) * gate * (1.0 + preact * (1.0 - gate))
    ).astype(BF)
    pre_s[...] = pre_grad

    def weight_rows(step, _):
        span = pl.ds(pl.multiple_of(step * GROUP * ch, GROUP * ch), GROUP * ch)
        d_s[span, :] = lax.dot_general(
            g_s[:, span], pre_s[...], (((0,), (0,)), ((), ())),
            preferred_element_type=F32,
        )
        return 0

    piece = 2 * half
    extra = PIECES * piece - padded * ch
    if extra:
        d_s[pl.ds(padded * ch, extra), :] = jnp.zeros((extra, ch), F32)

    def remote(src, dst, send, recv, peer):
        return pltpu.make_async_remote_copy(
            src_ref=src, dst_ref=dst, send_sem=send, recv_sem=recv,
            device_id=peer, device_id_type=MESH,
        )

    def at(start, size):
        return pl.ds(pl.multiple_of(start, 16), size)

    def core_sum(p):
        return remote(
            d_s.at[at(p * piece + (1 - c) * half, half)], r1.at[at(p * half, half)],
            c1s.at[p], c1r.at[p], core_peer,
        )

    def y_sum(p, k):
        slot = p * (near - 1) + k
        part = at(slot * quarter, quarter)
        return remote(s2.at[part], r2.at[part], y1s.at[slot], y1r.at[slot], y_peers[k])

    def z_sum(p, k):
        slot = p * (far - 1) + k
        part = at(slot * r, r)
        return remote(s3.at[part], r3.at[part], z1s.at[slot], z1r.at[slot], z_peers[k])

    def z_share(p, k):
        slot = p * (far - 1) + k
        part = at(p * piece + c * half + y * quarter + z * r, r)
        return remote(og.at[part], og.at[part], z2s.at[slot], z2r.at[slot], z_peers[k])

    def y_share(p, k):
        slot = p * (near - 1) + k
        part = at(p * piece + c * half + y * quarter, quarter)
        return remote(og.at[part], og.at[part], y2s.at[slot], y2r.at[slot], y_peers[k])

    def core_share(p):
        part = at(p * piece + c * half, half)
        return remote(og.at[part], og.at[part], c2s.at[p], c2r.at[p], core_peer)

    def out_copies(p):
        copies = []
        for source, to, count in (
            (0, 0, middle), (middle, middle + 1, middle), (others, middle, 1)
        ):
            first, last = max(source * ch, p * piece), min((source + count) * ch, (p + 1) * piece)
            if first < last:
                copies.append(
                    pltpu.make_async_copy(
                        og.at[pl.ds(first, last - first)],
                        gw_ref.at[pl.ds(first + (to - source) * ch, last - first)],
                        o_sem.at[3 * p + len(copies)],
                    )
                )
        return copies

    def after_core(p):
        core_sum(p).wait_recv()
        for k in range(near - 1):
            yy = around(y, k + 1, near)
            s2[at((p * (near - 1) + k) * quarter, quarter), :] = (
                d_s[at(p * piece + c * half + yy * quarter, quarter), :]
                + r1[at(p * half + yy * quarter, quarter), :]
            ).astype(BF)
            y_sum(p, k).start()
        b_s[at(p * quarter, quarter), :] = (
            d_s[at(p * piece + c * half + y * quarter, quarter), :]
            + r1[at(p * half + y * quarter, quarter), :]
        )

    def after_y(p):
        for k in range(near - 1):
            y_sum(p, k).wait_recv()
        total = b_s[at(p * quarter, quarter), :]
        for k in range(near - 1):
            total += r2[at((p * (near - 1) + k) * quarter, quarter), :].astype(F32)
        b_s[at(p * quarter, quarter), :] = total
        for k in range(far - 1):
            zz = around(z, k + 1, far)
            s3[at((p * (far - 1) + k) * r, r), :] = b_s[at(p * quarter + zz * r, r), :].astype(BF)
            z_sum(p, k).start()

    def after_z(p):
        for k in range(far - 1):
            z_sum(p, k).wait_recv()
        total = b_s[at(p * quarter + z * r, r), :]
        for k in range(far - 1):
            total += r3[at((p * (far - 1) + k) * r, r), :].astype(F32)
        og[at(p * piece + c * half + y * quarter + z * r, r), :] = total.astype(BF)
        for k in range(far - 1):
            z_share(p, k).start()

    def after_z_share(p):
        for k in range(far - 1):
            z_share(p, k).wait_recv()
        for k in range(near - 1):
            y_share(p, k).start()

    def after_y_share(p):
        for k in range(near - 1):
            y_share(p, k).wait_recv()
        core_share(p).start()

    def after_core_share(p):
        core_share(p).wait_recv()
        for copy in out_copies(p):
            copy.start()

    tacc[...] = jnp.zeros_like(tacc)

    def table_rows(start, count):
        span = pl.ds(pl.multiple_of(start * ch, ch), count * ch)
        spread = lax.dot_general(
            pre_s[...], w_s[span, :], (((1,), (1,)), ((), ())), preferred_element_type=F32
        )
        picks, parts = [], []
        for i in range(count):
            o = start + i
            upper = idxb[o] >= lo_rows
            term = spread[:, i * ch : (i + 1) * ch]
            parts.append(
                jnp.concatenate(
                    [jnp.where(upper, 0.0, term).astype(BF), jnp.where(upper, term, 0.0).astype(BF)],
                    axis=1,
                )
            )
            hit = iota_s[...].reshape(lo_rows // 16, 16, sites) == lo16[o][None]
            picks.append(jnp.where(hit, one, zero).reshape(lo_rows, sites))
        tacc[...] += jnp.dot(
            jnp.concatenate(picks, axis=1),
            jnp.concatenate(parts, axis=0),
            preferred_element_type=F32,
        )
        return 0

    def send_back():
        bs[...] = tacc[pl.ds(lo_rows - sides * halo, sides * halo), pl.ds(ch, ch)].astype(BF)
        for k in range(sides):

            @pl.when(exists(me - side_distance(k)))
            def _(k=k):
                back_copy(k).start()

    def finish_rows():
        for k in range(sides):

            @pl.when(exists(me + side_distance(k)))
            def _(k=k):
                back_copy(k).wait_recv()

        scattered = lax.dot_general(
            pre_s[...], w_s[pl.ds(others * ch, ch), :], (((1,), (1,)), ((), ())),
            preferred_element_type=F32,
        )
        for k in range(sides):
            scattered += jnp.dot(
                export_picks(k), br[pl.ds(k * halo, halo), :], preferred_element_type=F32
            )
        own = jnp.concatenate(
            [tacc[:, pl.ds(0, ch)], tacc[pl.ds(0, sites - lo_rows), pl.ds(ch, ch)]], axis=0
        )
        alive = jnp.where(idxb[others] >= 0, 1.0, 0.0)
        din_ref[...] = (alive * (cot_ref[...].astype(F32) + own + scattered)).astype(BF)
        pltpu.make_async_copy(din_ref, din_hbm, res_sem.at[1]).start()

    steps = padded // GROUP
    done = 0
    for p in range(PIECES):
        need = min(steps, -(-(p + 1) * piece // (GROUP * ch)))
        if need > done:
            lax.fori_loop(done, need, weight_rows, 0)
            done = need
        core_sum(p).start()
    for p in range(PIECES):
        after_core(p)
    cuts = [min(others, cut) for cut in (12, 20, others)]
    each_span(table_rows, 0, cuts[0])
    after_y(0)
    each_span(table_rows, cuts[0], cuts[1])
    for p in range(1, PIECES):
        after_y(p)
    each_span(table_rows, cuts[1], cuts[2])
    send_back()
    for p in range(PIECES):
        after_z(p)
    after_z_share(0)
    finish_rows()
    for p in range(1, PIECES):
        after_z_share(p)
    for p in range(PIECES):
        after_y_share(p)
    for p in range(PIECES):
        after_core_share(p)

    for k in range(sides):

        @pl.when(exists(me + side_distance(k)))
        def _(k=k):
            halo_copy(k).wait_send()

        @pl.when(exists(me - side_distance(k)))
        def _(k=k):
            back_copy(k).wait_send()

    for p in range(PIECES):
        core_sum(p).wait_send()
        for k in range(near - 1):
            y_sum(p, k).wait_send()
            y_share(p, k).wait_send()
        for k in range(far - 1):
            z_sum(p, k).wait_send()
            z_share(p, k).wait_send()
        core_share(p).wait_send()
        for copy in out_copies(p):
            copy.wait()
    out_copy_rows.wait()
    pltpu.make_async_copy(din_ref, din_hbm, res_sem.at[1]).wait()


def body(x, w, cot, counts, plan, exports):
    n = lax.axis_size("gx")
    sites, ch = x.shape
    offsets = w.shape[0]
    padded = -(-offsets // GROUP) * GROUP
    sides, halo = exports.shape[1:]
    middle = offsets // 2
    near, far = grid_of(n)
    r = rows_each(n, padded * ch)
    quarter = far * r
    half = near * quarter
    pieces = pieces_of(n, padded * ch)
    total = pieces * 2 * half
    lo_rows = (sites + sides * halo) // 2
    anyspace = pl.BlockSpec(memory_space=pl.ANY)
    dma = pltpu.SemaphoreType.DMA
    y_slots = max(1, pieces * (near - 1))
    z_slots = max(1, pieces * (far - 1))
    out, din, gw = pl.pallas_call(
        functools.partial(kernel, n, r, offsets, padded),
        out_shape=(
            jax.ShapeDtypeStruct((sites, ch), BF),
            jax.ShapeDtypeStruct((sites, ch), BF),
            jax.ShapeDtypeStruct((offsets * ch, ch), BF),
        ),
        in_specs=[anyspace] * 6,
        out_specs=(anyspace,) * 3,
        scratch_shapes=[
            pltpu.VMEM((sites, ch), BF),
            pltpu.VMEM((sites, ch), BF),
            pltpu.VMEM((offsets, sites), jnp.int32),
            pltpu.VMEM((1, sides, halo), jnp.int32),
            pltpu.VMEM((sites, ch), BF),
            pltpu.VMEM((sites, ch), BF),
            dma((4,)),
            dma((2,)),
            pltpu.VMEM((padded * ch, ch), BF),
            pltpu.VMEM((-(-padded // 8) * 8, sites), F32),
            pltpu.VMEM((sites // 2, 2 * ch), BF),
            pltpu.VMEM((sides * halo, ch), BF),
            pltpu.VMEM((padded, sites, ch), F32),
            pltpu.VMEM((padded, sites, ch), BF),
            pltpu.VMEM((padded, 16, sites), BF),
            pltpu.VMEM((lo_rows, sites), BF),
            pltpu.VMEM((sites, padded * ch), BF),
            pltpu.VMEM((sites, ch), F32),
            pltpu.VMEM((total, ch), F32),
            pltpu.VMEM((pieces * half, ch), F32),
            pltpu.VMEM((y_slots * quarter, ch), BF),
            pltpu.VMEM((y_slots * quarter, ch), BF),
            pltpu.VMEM((pieces * quarter, ch), F32),
            pltpu.VMEM((z_slots * r, ch), BF),
            pltpu.VMEM((z_slots * r, ch), BF),
            pltpu.VMEM((total, ch), BF),
            pltpu.VMEM((sides * halo, ch), BF),
            pltpu.VMEM((lo_rows, 2 * ch), F32),
            pltpu.VMEM((sides * halo, ch), BF),
            pltpu.VMEM((sides * halo, ch), BF),
            pltpu.VMEM((sites, ch), BF),
            dma((3,)),
            dma((3 * pieces,)),
            dma((sides,)), dma((sides,)), dma((sides,)), dma((sides,)),
            dma((pieces,)), dma((pieces,)),
            dma((y_slots,)), dma((y_slots,)),
            dma((z_slots,)), dma((z_slots,)),
            dma((z_slots,)), dma((z_slots,)),
            dma((y_slots,)), dma((y_slots,)),
            dma((pieces,)), dma((pieces,)),
        ],
        compiler_params=pltpu.CompilerParams(
            collective_id=0, has_side_effects=True, vmem_limit_bytes=60 * 1024 * 1024
        ),
    )(x, w.reshape(offsets * ch, ch), cot, counts, plan, exports)
    out, din, gw = pl.pallas_call(
        functools.partial(finish, 3),
        out_shape=(
            jax.ShapeDtypeStruct((sites, ch), BF),
            jax.ShapeDtypeStruct((sites, ch), BF),
            jax.ShapeDtypeStruct((offsets * ch, ch), F32),
        ),
        in_specs=[anyspace] * 3,
        out_specs=(anyspace,) * 3,
        scratch_shapes=[
            pltpu.VMEM((2, sites, ch), BF),
            pltpu.VMEM((offsets * ch, ch), BF),
            pltpu.VMEM((offsets * ch, ch), F32),
            dma((2,)), dma((2,)), dma((3,)), dma((3,)),
        ],
        compiler_params=pltpu.CompilerParams(vmem_limit_bytes=60 * 1024 * 1024),
    )(out, din, gw)
    return out, din, gw.reshape(offsets, ch, ch)


def solution(mesh):
    return jax.shard_map(
        body,
        mesh=mesh,
        in_specs=(
            P(("groups", "gx"), None),
            P(),
            P(("groups", "gx"), None),
            P(("groups", "gx")),
            P(None, ("groups", "gx")),
            P(("groups", "gx"), None, None),
        ),
        out_specs=(P(("groups", "gx"), None), P(("groups", "gx"), None), P("groups", None, None)),
        check_vma=False,
    )
```
